32 devices in a mesh: fsdp: 16 (over z, x, core), tensor: 2 (over y).
Axes of the slice: x: 2, y: 2, z: 4, core: 2. Of those that a mesh axis runs over, the one named last changes fastest.
Arguments:
- tokens: bfloat16 [6144, 8192], P(('fsdp', 'tensor'))
- gain: bfloat16 [8192], replicated, may hold values from 0.5 to 1.5
- kv_weight: bfloat16 [8192, 2048], P('fsdp', 'tensor'), may hold values from -0.09375 to 0.09375
- block_mask: int32 [64, 16], P('fsdp', 'tensor'), may hold values from 0 to 1
- cotangent: bfloat16 [6144, 2048], P('fsdp', 'tensor'), may hold values from -0.078125 to 0.078125
Outputs:
- projected: bfloat16 [6144, 2048], P('fsdp', 'tensor')
- weight_grad: float32 [8192, 2048], P('fsdp', 'tensor')
The draws below stay inside these ranges and needn't reach their ends.
All inputs are finite; a program needn't handle non-finite values.
Results may differ from the reference program's by a relative error of at most 0.005.
Values may be sent and summed in bfloat16 or wider, within the bound.
No kernel may reach another device: no remote copies, remote signals or barrier semaphores. Data moves between devices by JAX's collectives and lax.ppermute only.
A program may use at most 128 MiB of HBM per device.

```python
import math
import jax
import jax.numpy as jnp
from jax import lax

D = 8192
KVW = 2048
BLOCK = 128
TOKENS = 6144


def draw_tokens(key, part):
    first, second = jax.random.split(key, 2)
    scale = jnp.exp(jax.random.uniform(second, (TOKENS, 1), jnp.float32) * math.log(10.0))
    values = jax.random.normal(first, (TOKENS, D), jnp.float32) * scale
    return values.astype(jnp.bfloat16)


def draw_block_mask(key, part):
    first, second = jax.random.split(jax.random.fold_in(key, 17))
    density = jax.random.randint(first, (D // BLOCK, 1), 20, 81)
    trial = jax.random.randint(second, (D // BLOCK, KVW // BLOCK), 0, 100)
    return jnp.where(trial < density, 1, 0).astype(jnp.int32)


def shard_levels(own_key, shape, cuts, least, top_value):
    level, own = 1.0, jax.random.fold_in(own_key, 6)
    for position, shards_of in cuts:
        draws = jnp.exp(jax.random.uniform(jax.random.fold_in(own, position), (shards_of,), jnp.float32, least / len(cuts), top_value / len(cuts)))
        level = level * jnp.repeat(draws, shape[position] // shards_of).reshape([-1 if axis == position else 1 for axis in range(len(shape))])
    return level


def gaussian(rng, dims, scale, reach, cuts=(), dtype=jnp.bfloat16):
    values = jax.random.normal(rng, dims, jnp.float32) * scale
    if len(cuts) > 0:
        values = shard_levels(rng, dims, cuts, -0.22, 0.18) * values
    return jnp.clip(values, min=-reach, max=reach).astype(dtype)


def setup_inputs(seed: int = 0) -> dict:
    keys = jax.random.split(jax.random.key(seed), 6)
    tokens = draw_tokens(jax.random.fold_in(keys[5], 71), 0)
    gain = jnp.clip(1.0 + 0.1 * jax.random.normal(keys[1], (D,), jnp.float32), 0.5, 1.5).astype(jnp.bfloat16)
    kv_weight = gaussian(keys[2], (D, KVW), (D // 2) ** -0.5, 0.09375, ((0, 16), (1, 2)))
    block_mask = draw_block_mask(jax.random.fold_in(keys[5], 71), 0)
    cotangent = gaussian(keys[4], (TOKENS, KVW), TOKENS ** -0.5, 0.078125, ((0, 16), (1, 2)))
    return {"tokens": tokens, "gain": gain, "kv_weight": kv_weight, "block_mask": block_mask, "cotangent": cotangent}


def expand_mask(block_mask):
    wide = jnp.repeat(block_mask, BLOCK, axis=0)
    return jnp.repeat(wide, BLOCK, axis=1).astype(jnp.float32)

def reference(tokens, gain, kv_weight, block_mask, cotangent):
    values = tokens.astype(jnp.float32)
    square = lax.optimization_barrier(jnp.mean(values * values, axis=-1, keepdims=True))
    normed = (values * lax.rsqrt(square + 1e-05) * gain.astype(jnp.float32)).astype(jnp.bfloat16)
    full_mask = expand_mask(block_mask)
    masked = (kv_weight.astype(jnp.float32) * full_mask).astype(jnp.bfloat16)
    projected = jnp.dot(normed, masked, preferred_element_type=jnp.float32).astype(jnp.bfloat16)
    product = lax.dot_general(normed, cotangent, (((0,), (0,)), ((), ())), preferred_element_type=jnp.float32)
    weight_grad = product * full_mask
    return (projected, weight_grad)
```

```python
import functools

import jax
import jax.numpy as jnp
import numpy as np
from jax import lax
from jax.experimental import pallas as pl
from jax.experimental.pallas import tpu as pltpu
from jax.sharding import PartitionSpec as P

BF = jnp.bfloat16
F32 = jnp.float32


def orders(depth):
    order = np.array([sorted(range(depth), key=lambda d: (-abs(d - z), -d)) for z in range(depth)])
    return order, np.argsort(order, axis=1)


def norm_kernel(layers, width, index, tokens, gain, *outs):
    values = tokens[...].astype(F32)
    scale = lax.rsqrt(jnp.mean(values * values, axis=-1, keepdims=True) + 1e-05)
    for r in range(4):
        for k in range(layers):
            at = pl.ds(pl.multiple_of(index[r * layers + k] * width, width), width)
            part = tokens[:, at].astype(F32) * scale * gain[:, at].astype(F32)
            outs[r][k] = part.astype(BF)


def normalize(tokens, gain, index, layers, tile=64):
    rows, features = tokens.shape
    width = features // (4 * layers)
    return pl.pallas_call(
        functools.partial(norm_kernel, layers, width),
        out_shape=[jax.ShapeDtypeStruct((layers, rows, width), BF)] * 4,
        grid_spec=pltpu.PrefetchScalarGridSpec(
            num_scalar_prefetch=1,
            grid=(rows // tile,),
            in_specs=[
                pl.BlockSpec((tile, features), lambda i, s: (i, 0)),
                pl.BlockSpec((1, features), lambda i, s: (0, 0)),
            ],
            out_specs=[pl.BlockSpec((layers, tile, width), lambda i, s: (0, i, 0))] * 4,
        ),
        compiler_params=pltpu.CompilerParams(vmem_limit_bytes=32 * 2**20),
        name="normalize",
    )(index, tokens, gain.reshape(1, features))


def apply_mask(panel, mask):
    rows, cols = panel.shape
    mrows, mcols = mask.shape
    shaped = panel.reshape(mrows, rows // mrows, mcols, cols // mcols)
    kept = shaped * mask[:, None, :, None].astype(panel.dtype)
    return kept.reshape(rows, cols)


def pick(arrays, which, values):
    values = sorted(set(int(v) for v in values))
    out = arrays[values[0]]
    for v in values[1:]:
        out = jnp.where(which == v, arrays[v], out)
    return out


def per_device(tokens, gain, kv_weight, block_mask, cotangent):
    group, teams = lax.axis_size("fsdp"), lax.axis_size("tensor")
    layers = group // 4
    f, t = lax.axis_index("fsdp"), lax.axis_index("tensor")
    z, x, c = f // 4, (f // 2) % 2, f % 2
    rows, features = tokens.shape
    width = features // group
    cols = kv_weight.shape[1]
    order, place = orders(layers)

    def over_core(a):
        return lax.ppermute(a, "fsdp", [(i, i ^ 1) for i in range(group)])

    def over_x(a):
        return lax.ppermute(a, "fsdp", [(i, i ^ 2) for i in range(group)])

    def over_y(a):
        return [
            lax.ppermute(a, "tensor", [(i, (i + s) % teams) for i in range(teams)])
            for s in range(1, teams)
        ]

    def over_z(a, pairs):
        return lax.ppermute(a, "fsdp", [(4 * p + i, 4 * q + i) for p, q in pairs for i in range(4)])

    def turn(a):
        parts = a.reshape(teams, rows, a.shape[1])
        if teams == 2:
            back = jnp.concatenate([parts[1:], parts[:1]])
            return jnp.where(t == 0, jnp.concatenate([parts[:1], parts[1:]]), back).reshape(a.shape)
        return parts[(t - jnp.arange(teams)) % teams].reshape(a.shape)

    cot = turn(cotangent)
    cot_x = over_x(cot)
    cot_pair = over_core(jnp.concatenate([cot, cot_x]))
    half = cot.shape[0]

    masked = apply_mask(kv_weight, block_mask)
    ups, downs = [masked], [masked]
    for s in range(1, layers):
        ups.append(over_z(ups[-1], [(p, p + 1) for p in range(s - 1, layers - 1)]))
        downs.append(over_z(downs[-1], [(p, p - 1) for p in range(1, layers - s + 1)]))

    rank = jnp.asarray(order)[z]
    index = jnp.concatenate(
        [rank * 4 + (x ^ rx) * 2 + (c ^ rc) for rx in range(2) for rc in range(2)]
    ).astype(jnp.int32)
    own, core, far, diag = normalize(tokens, gain, index, layers)

    sets = [(0, 1), (1, 2), (2, layers)]
    normed = [None] * layers
    for lo, hi in sets:
        got = over_core(jnp.stack([core[lo:hi], diag[lo:hi]]))
        near = jnp.concatenate([own[lo:hi], got[0]], axis=1)
        cross = over_x(jnp.concatenate([far[lo:hi], got[1]], axis=1))
        pieces = []
        for part in [near, cross]:
            pieces.append([part] + over_y(part))
        for k in range(lo, hi):
            blocks = []
            for arrived in pieces:
                for core_rel in range(2):
                    for piece in arrived:
                        blocks.append(piece[k - lo, core_rel * rows:(core_rel + 1) * rows])
            normed[k] = jnp.concatenate(blocks)
    cots = jnp.concatenate([cot, cot_pair[:half], cot_x, cot_pair[half:]])

    terms = [
        lax.dot_general(n, cots, (((0,), (0,)), ((), ())), preferred_element_type=F32) for n in normed
    ]
    up = down = jnp.zeros((width, cols), BF)
    for s in range(1, layers):
        d = layers - s
        kp = [place[i, min(i + d, layers - 1)] for i in range(layers)]
        km = [place[i, max(i - d, 0)] for i in range(layers)]
        vp = [kp[i] for i in range(layers) if i + d < layers]
        vm = [km[i] for i in range(layers) if i - d >= 0]
        send_up = (pick(terms, jnp.asarray(kp)[z], vp) + up.astype(F32)).astype(BF)
        send_down = (pick(terms, jnp.asarray(km)[z], vm) + down.astype(F32)).astype(BF)
        up = over_z(send_up, [(p, p + 1) for p in range(s)])
        down = over_z(send_down, [(p, p - 1) for p in range(layers - s, layers)])
    weight_grad = apply_mask(terms[layers - 1] + up.astype(F32) + down.astype(F32), block_mask)

    total = jnp.dot(normed[layers - 1], masked, preferred_element_type=F32)
    for s in range(1, layers):
        ku = [place[i, max(i - s, 0)] for i in range(layers)]
        kd = [place[i, min(i + s, layers - 1)] for i in range(layers)]
        vu = [ku[i] for i in range(layers) if i - s >= 0]
        vd = [kd[i] for i in range(layers) if i + s < layers]
        if 2 * s >= layers:
            both = ups[s] + downs[s]
            which = jnp.where(z >= s, jnp.asarray(ku)[z], jnp.asarray(kd)[z])
            total += jnp.dot(pick(normed, which, vu + vd), both, preferred_element_type=F32)
        else:
            total += jnp.dot(pick(normed, jnp.asarray(ku)[z], vu), ups[s], preferred_element_type=F32)
            total += jnp.dot(pick(normed, jnp.asarray(kd)[z], vd), downs[s], preferred_element_type=F32)
    total = total.reshape(2, 2, half, cols)
    sums = total[:, 0] + over_core(total[:, 1])
    projected = turn((sums[0] + over_x(sums[1].astype(BF)).astype(F32)).astype(BF))
    return (projected, weight_grad)


def solution(mesh):
    return jax.shard_map(
        per_device,
        mesh=mesh,
        in_specs=(
            P(("fsdp", "tensor"), None),
            P(),
            P("fsdp", "tensor"),
            P("fsdp", "tensor"),
            P("fsdp", "tensor"),
        ),
        out_specs=(P("fsdp", "tensor"), P("fsdp", "tensor")),
        check_vma=False,
    )
```

```python
import functools

import jax
import jax.numpy as jnp
import numpy as np
from jax import lax
from jax.experimental import pallas as pl
from jax.experimental.pallas import tpu as pltpu
from jax.sharding import PartitionSpec as P

BF = jnp.bfloat16
F32 = jnp.float32
PARTS = 1


def orders(depth):
    order = np.array([sorted(range(depth), key=lambda d: (-abs(d - z), -d)) for z in range(depth)])
    return order, np.argsort(order, axis=1)


def lookup(table, where):
    out = jnp.int32(int(table[0]))
    for i in range(1, len(table)):
        out = jnp.where(where == i, jnp.int32(int(table[i])), out)
    return out


def norm_kernel(order, width, spot, tokens, gain, held, own, first, later, far, token):
    layers = len(order)
    values = tokens[...].astype(F32)
    scale = lax.rsqrt(jnp.mean(values * values, axis=-1, keepdims=True) + 1e-05)
    for k in range(layers):
        layer = lookup(order[:, k], spot[0]) * 4
        outs = [(own.at[k], 0, 0), (first.at[0] if k == 0 else later.at[0, k - 1], 0, 1)]
        outs += [(far.at[k], 1, 0), (first.at[1] if k == 0 else later.at[1, k - 1], 1, 1)]
        for out, rx, rc in outs:
            place = layer + jnp.bitwise_xor(spot[1], rx) * 2 + jnp.bitwise_xor(spot[2], rc)
            at = pl.ds(pl.multiple_of(place * width, width), width)
            part = tokens[:, at].astype(F32) * scale * gain[:, at].astype(F32)
            out[...] = part.astype(BF)
    token[...] = jnp.zeros_like(token)


def normalize(tokens, gain, spot, held, order, tile=64):
    layers = len(order)
    rows, features = tokens.shape
    width = features // (4 * layers)
    shapes = [(layers, rows, width), (2, rows, width), (2, layers - 1, rows, width), (layers, rows, width)]
    blocks = [pl.BlockSpec((layers, tile, width), lambda i: (0, i, 0))]
    blocks.append(pl.BlockSpec((2, tile, width), lambda i: (0, i, 0)))
    blocks.append(pl.BlockSpec((2, layers - 1, tile, width), lambda i: (0, 0, i, 0)))
    blocks.append(blocks[0])
    return pl.pallas_call(
        functools.partial(norm_kernel, order, width),
        out_shape=[jax.ShapeDtypeStruct(shape, BF) for shape in shapes] + [jax.ShapeDtypeStruct((8, 128), F32)],
        grid=(rows // tile,),
        in_specs=[
            pl.BlockSpec(memory_space=pltpu.SMEM),
            pl.BlockSpec((tile, features), lambda i: (i, 0)),
            pl.BlockSpec((1, features), lambda i: (0, 0)),
            pl.BlockSpec(memory_space=pl.ANY),
        ],
        out_specs=blocks + [pl.BlockSpec((8, 128), lambda i: (0, 0))],
        compiler_params=pltpu.CompilerParams(vmem_limit_bytes=60 * 2**20),
        name="normalize",
    )(spot, tokens, gain.reshape(1, features), held)


def whole(shape):
    return pl.BlockSpec(shape, lambda i: (0,) * len(shape))


def at(shape, *where):
    return pl.BlockSpec(shape, lambda i: where)


HELD = pl.BlockSpec(memory_space=pl.ANY)
SCALARS = pl.BlockSpec(memory_space=pltpu.SMEM)


class Line:
    def __init__(self):
        self.token = None

    def call(self, name, kernel, ins, outs, wait=(), alias=None, grid=(1,), cost=(0, 1)):
        held = list(wait) + ([] if self.token is None else [self.token])
        n_in, n_held, n_out = len(ins), len(held), len(outs)

        def body(*refs):
            refs, token = refs[:-1], refs[-1]
            kernel(*refs[:n_in], *refs[n_in + n_held:])
            token[...] = jnp.zeros_like(token)

        result = pl.pallas_call(
            body,
            out_shape=[o for o, _ in outs] + [jax.ShapeDtypeStruct((8, 128), F32)],
            grid=grid,
            in_specs=[spec for _, spec in ins] + [HELD] * n_held,
            out_specs=[spec for _, spec in outs] + [whole((8, 128))],
            input_output_aliases=alias or {},
            compiler_params=pltpu.CompilerParams(vmem_limit_bytes=32 * 2**20),
            cost_estimate=pl.CostEstimate(flops=cost[0], bytes_accessed=cost[1], transcendentals=0),
            name=name,
        )(*[a for a, _ in ins], *held)
        self.token = result[-1]
        return result[:-1]

    def gate(self, *arrays):
        outs = [(jax.ShapeDtypeStruct(a.shape, a.dtype), HELD) for a in arrays]
        alias = {i: i for i in range(len(arrays))}
        out = self.call("gate", lambda *refs: None, [(a, HELD) for a in arrays], outs, alias=alias)
        return out if len(out) > 1 else out[0]

    def join(self, name, pieces, **more):
        rows = sum(block[-2] for _, block, _ in pieces)
        cols = pieces[0][1][-1]

        def kernel(*refs):
            ins, out = refs[:-1], refs[-1]
            row = 0
            for ref in ins:
                flat = ref.shape[-2:]
                out[row:row + flat[0], :] = ref[...].reshape(flat)
                row += flat[0]

        shape = jax.ShapeDtypeStruct((rows, cols), pieces[0][0].dtype)
        ins = [(a, at(block, *where)) for a, block, where in pieces]
        return self.call(name, kernel, ins, [(shape, whole((rows, cols)))], **more)[0]


def per_device(tokens, gain, kv_weight, block_mask, cotangent):
    group, teams = lax.axis_size("fsdp"), lax.axis_size("tensor")
    layers = group // 4
    f, t = lax.axis_index("fsdp"), lax.axis_index("tensor")
    z, x, c = f // 4, (f // 2) % 2, f % 2
    rows, features = tokens.shape
    width = features // group
    cols = kv_weight.shape[1]
    order, place = orders(layers)
    line = Line()

    def over_core(a):
        return lax.ppermute(a, "fsdp", [(i, i ^ 1) for i in range(group)])

    def over_x(a):
        return lax.ppermute(a, "fsdp", [(i, i ^ 2) for i in range(group)])

    def over_y(a):
        return [
            lax.ppermute(a, "tensor", [(i, (i + s) % teams) for i in range(teams)])
            for s in range(1, teams)
        ]

    def over_z(a, pairs):
        return lax.ppermute(a, "fsdp", [(4 * p + i, 4 * q + i) for p, q in pairs for i in range(4)])

    spot = (jnp.stack([z, x, c, t]).astype(jnp.int32), SCALARS)

    def turn_kernel(spot, a, out):
        for i in range(teams):
            j = lax.rem(spot[3] + teams - i, teams)
            out[i * rows:(i + 1) * rows, :] = a[pl.ds(pl.multiple_of(j * rows, rows), rows), :]

    own_shape = cotangent.shape
    cot = line.call(
        "turn", turn_kernel, [spot, (cotangent, whole(own_shape))],
        [(jax.ShapeDtypeStruct(own_shape, BF), whole(own_shape))],
    )[0]
    cot_x = over_x(cot)

    cot_core = over_core(cot)

    own, first, later, far, line.token = normalize(tokens, gain, spot[0], line.token, order)
    first = over_core(first)
    later = over_core(later)
    cot_core = line.gate(cot_core)

    mrows, mcols = block_mask.shape
    tall, wide = width // mrows, cols // mcols

    def mask_kernel(mask, a, out):
        for i in range(mrows):
            for j in range(mcols):
                spot = (slice(i * tall, (i + 1) * tall), slice(j * wide, (j + 1) * wide))
                out[spot] = (a[spot].astype(F32) * mask[i, j].astype(F32)).astype(BF)

    panel = (width, cols)
    masked = line.call(
        "mask", mask_kernel, [(block_mask, SCALARS), (kv_weight, whole(panel))],
        [(jax.ShapeDtypeStruct(panel, BF), whole(panel))],
    )[0]
    up_weight = [masked, over_z(masked, [(p, p + 1) for p in range(layers - 1)])]
    down_weight = [masked, over_z(masked, [(p, p - 1) for p in range(1, layers)])]

    one, two = (1, rows, width), (1, 1, rows, width)

    def near_of(k):
        return [(own, one, (k, 0, 0)), (first, one, (0, 0, 0)) if k == 0 else (later, two, (0, k - 1, 0, 0))]

    def cross_of(k):
        return [(far, one, (k, 0, 0)), (first, one, (1, 0, 0)) if k == 0 else (later, two, (1, k - 1, 0, 0))]

    normed, terms = [None] * layers, [None] * layers
    pair = (2 * rows, width)
    cross_0 = over_x(line.join("cross", cross_of(0)))
    near_0 = line.join("near", near_of(0))
    near_y = over_y(near_0)

    cross_1 = line.join("cross", cross_of(1))
    rest = line.join("cross", [p for k in range(2, layers) for p in cross_of(k)])

    cut = (own_shape[0] // 2, cols)

    def split_kernel(a, low, high):
        low[...] = a[:cut[0]]
        high[...] = a[cut[0]:]

    parts = line.call(
        "split", split_kernel, [(cot_x, whole(own_shape))], [(jax.ShapeDtypeStruct(cut, BF), whole(cut))] * 2
    )
    parts = [over_core(part) for part in parts]

    def add_terms(k, pieces):
        normed[k] = line.join("rows", pieces)
        terms[k] = lax.dot_general(
            normed[k], cots, (((0,), (0,)), ((), ())), preferred_element_type=F32
        )

    def send(s, h, halves, sums):
        d = layers - s
        ups, downs = [(p, p + 1) for p in range(s)], [(p, p - 1) for p in range(layers - s, layers)]
        ku = [place[i, i + d] if i + d < layers else -1 for i in range(layers)]
        kd = [place[i, i - d] if i - d >= 0 else -1 for i in range(layers)]
        single = 2 * s <= layers
        ways = [[max(u, v) for u, v in zip(ku, kd)]] if single else [ku, kd]
        known = sorted({int(k) for w in ways for k in w if k >= 0})
        shape = (width // halves, cols)

        def kernel(spot, *refs):
            which = [lookup(w, spot[0]) for w in ways]
            inside = [
                jnp.where((spot[0] >= 1) & (spot[0] < s), 1, 0),
                jnp.where((spot[0] < layers - 1) & (spot[0] >= layers - s), 1, 0),
            ]
            held, arrived, outs = refs[:len(known)], refs[len(known):len(known) + len(sums)], refs[len(known) + len(sums):]
            for w, out in enumerate(outs):
                for i, k in enumerate(known):
                    if k not in ways[w]:
                        continue

                    @pl.when(which[w] == k)
                    def _():
                        total = held[i][...]
                        if len(arrived) == 1:
                            total += jnp.where(inside[0] + inside[1] > 0, arrived[0][...].astype(F32), 0.0)
                        elif arrived and single:
                            total += jnp.where(inside[0] > 0, arrived[0][...].astype(F32), 0.0)
                            total += jnp.where(inside[1] > 0, arrived[1][...].astype(F32), 0.0)
                        elif arrived:
                            total += jnp.where(inside[w] > 0, arrived[w][...].astype(F32), 0.0)
                        out[...] = total.astype(BF)

                @pl.when(which[w] < 0)
                def _():
                    out[...] = jnp.zeros_like(out)

        ins = [spot] + [(terms[k], at(shape, h, 0)) for k in known] + [(a, whole(shape)) for a in sums]
        outs = [(jax.ShapeDtypeStruct(shape, BF), whole(shape))] * len(ways)
        out = line.call("sums", kernel, ins, outs)
        if 2 * s < layers - 1:
            return [over_z(out[0], ups + downs)]
        return [over_z(out[0], ups), over_z(out[-1], downs)]

    def gather(near, near_y, cross, cross_y, places=(0, 0)):
        blocks = [(a, pair, (places[0], 0)) for a in [near, *near_y]]
        return blocks + [(a, pair, (places[1], 0)) for a in [cross, *cross_y]]

    cross_0 = line.gate(cross_0)
    cross_y = over_y(cross_0)
    cross_1 = over_x(cross_1)
    pieces = [(a, (rows, cols), (i, 0)) for i in range(teams) for a in (cot, cot_core)]
    for i in range(teams):
        pieces.append((cot_x, (rows, cols), (i, 0)))
        pieces.append((parts[2 * i // teams], (rows, cols), (i % (teams // 2), 0)))
    cots = line.join("cotangents", pieces)
    up, down = line.gate(up_weight[1], down_weight[1])
    up_weight[1], down_weight[1] = up, down
    for s in range(2, layers - 1):
        up_weight.append(over_z(up_weight[-1], [(p, p + 1) for p in range(s - 1, layers - 1)]))
        down_weight.append(over_z(down_weight[-1], [(p, p - 1) for p in range(1, layers - s + 1)]))
    add_terms(0, gather(near_0, near_y, cross_0, cross_y))
    sums = [send(1, h, PARTS, []) for h in range(PARTS)]

    late, late_y = {}, {}

    def start_late(k):
        pieces = near_of(k) + ([(cross_1, pair, (0, 0))] if k == 1 else [(rest, pair, (k - 2, 0))])
        late[k] = line.join("late", pieces)
        late_y[k] = over_y(late[k])

    def end_late(k):
        add_terms(k, gather(late[k], late_y[k], late[k], late_y[k], (0, 1)))

    start_late(1)
    rest = over_x(line.gate(rest))
    end_late(1)

    def last_kernel(spot, up, down, out):
        @pl.when(spot[0] == layers - 2)
        def _():
            out[...] = up[...]

        @pl.when(spot[0] != layers - 2)
        def _():
            out[...] = down[...]

    last = line.call(
        "last",
        last_kernel,
        [spot] + [(a, whole(panel)) for a in (up_weight[-1], down_weight[-1])],
        [(jax.ShapeDtypeStruct(panel, BF), whole(panel))],
    )[0]
    last = over_z(last, [(layers - 2, layers - 1), (1, 0)])
    for k in range(2, layers):
        start_late(k)
    for s in range(2, layers):
        sums = [send(s, h, PARTS, sums[h]) for h in range(PARTS)]
        end_late(s)

    def weight_of(d):
        spots = [int(order[i, d]) - i for i in range(layers)]
        options = {}
        for i, away in enumerate(spots):
            if abs(away) == layers - 1:
                options.setdefault("last", (last, []))[1].append(i)
            elif away > 0:
                options.setdefault(away, (down_weight[away], []))[1].append(i)
            else:
                options.setdefault(away, (up_weight[-away], []))[1].append(i)
        options = list(options.values())
        out = options[0][0]
        for arr, layers_of in options[1:]:
            hit = functools.reduce(jnp.logical_or, [z == i for i in layers_of])
            out = jnp.where(hit, arr, out)
        return out

    weight = [weight_of(k) for k in range(layers)]

    def project(side):
        def kernel(*refs):
            rows_of, weights, keep, send_out = refs[:layers], refs[layers:2 * layers], refs[-2], refs[-1]
            total = jnp.dot(rows_of[0][...], weights[0][...], preferred_element_type=F32)
            for k in range(1, layers):
                total += jnp.dot(rows_of[k][...], weights[k][...], preferred_element_type=F32)
            keep[...] = total[:rows]
            send_out[...] = total[rows:].astype(BF)

        ins = [(n, pl.BlockSpec(pair, lambda i: (side * teams + i, 0))) for n in normed]
        ins += [(w, whole((width, cols))) for w in weight]
        shape = (teams * rows, cols)
        outs = [(jax.ShapeDtypeStruct(shape, d), pl.BlockSpec((rows, cols), lambda i: (i, 0))) for d in (F32, BF)]
        cost = (0, 1)
        return line.call("project", kernel, ins, outs, grid=(teams,), cost=cost)

    full = (teams * rows, cols)

    def add_kernel(kept, sent, out):
        out[...] = (kept[...] + sent[...].astype(F32)).astype(BF)

    kept_x, sent_x = project(1)
    sent_x = over_core(sent_x)
    kept, sent = project(0)
    cross_sum = over_x(
        line.call(
            "cross_sum", add_kernel, [(kept_x, whole(full)), (sent_x, whole(full))],
            [(jax.ShapeDtypeStruct(full, BF), whole(full))],
        )[0]
    )
    sent = over_core(sent)

    half = width // PARTS

    def own_kernel(h):
        def kernel(mask, term, up, down, *refs):
            out = refs[-1]
            for i in range(half // tall):
                for j in range(mcols):
                    spot = (slice(i * tall, (i + 1) * tall), slice(j * wide, (j + 1) * wide))
                    total = term[spot] + up[spot].astype(F32) + down[spot].astype(F32)
                    out[spot] = total * mask[h * (half // tall) + i, j].astype(F32)
        return kernel

    weight_grad = None
    for h in range(PARTS):
        up, down = sums[h]
        ins = [(block_mask, SCALARS), (terms[layers - 1], at((half, cols), h, 0))]
        ins += [(up, whole((half, cols))), (down, whole((half, cols)))]
        alias = None
        if weight_grad is not None:
            ins.append((weight_grad, HELD))
            alias = {4: 0}
        outs = [(jax.ShapeDtypeStruct((width, cols), F32), at((half, cols), h, 0))]
        weight_grad = line.call("own_gradient", own_kernel(h), ins, outs, alias=alias)[0]

    def last_sum(spot, kept, sent, arrived, out):
        total = (kept[...] + sent[...].astype(F32) + arrived[...].astype(F32)).astype(BF)
        for i in range(teams):
            j = lax.rem(spot[3] + teams - i, teams)
            out[pl.ds(pl.multiple_of(j * rows, rows), rows), :] = total[i * rows:(i + 1) * rows]

    projected = line.call(
        "projected", last_sum, [spot] + [(a, whole(full)) for a in (kept, sent, cross_sum)],
        [(jax.ShapeDtypeStruct(full, BF), whole(full))],
    )[0]
    return (projected, weight_grad)


def solution(mesh):
    return jax.shard_map(
        per_device,
        mesh=mesh,
        in_specs=(
            P(("fsdp", "tensor"), None),
            P(),
            P("fsdp", "tensor"),
            P("fsdp", "tensor"),
            P("fsdp", "tensor"),
        ),
        out_specs=(P("fsdp", "tensor"), P("fsdp", "tensor")),
        check_vma=False,
    )
```

```python
import functools

import jax
import jax.numpy as jnp
import numpy as np
from jax import lax
from jax.experimental import pallas as pl
from jax.experimental.pallas import tpu as pltpu
from jax.sharding import PartitionSpec as P

BF = jnp.bfloat16
F32 = jnp.float32


def orders(depth):
    def rank(z):
        return lambda d: (-abs(d - z), abs(2 * d - depth + 1))

    order = np.array([sorted(range(depth), key=rank(z)) for z in range(depth)])
    return order, np.argsort(order, axis=1)


def lookup(table, where):
    out = jnp.int32(int(table[0]))
    for i in range(1, len(table)):
        out = jnp.where(where == i, jnp.int32(int(table[i])), out)
    return out


def lookup(table, where):
    out = jnp.int32(int(table[0]))
    for i in range(1, len(table)):
        out = jnp.where(where == i, jnp.int32(int(table[i])), out)
    return out


def spot():
    f = lax.axis_index("fsdp")
    return lax.div(f, 4), lax.rem(lax.div(f, 2), 2), lax.rem(f, 2), lax.axis_index("tensor")


def norm_kernel(order, width, tokens, gain, token, *outs):
    layers = len(order)
    z, x, c, _ = spot()
    values = tokens[...].astype(F32)
    scale = lax.rsqrt(jnp.mean(values * values, axis=-1, keepdims=True) + 1e-05)
    for k in range(layers):
        own, far, swap = outs[k], outs[layers + k], outs[2 * layers + k]
        layer = lookup(order[:, k], z) * 4
        for out, rx, rc in [(own, 0, 0), (swap.at[0], 0, 1), (far, 1, 0), (swap.at[1], 1, 1)]:
            place = layer + jnp.bitwise_xor(x, rx) * 2 + jnp.bitwise_xor(c, rc)
            at = pl.ds(pl.multiple_of(place * width, width), width)
            part = tokens[:, at].astype(F32) * scale * gain[:, at].astype(F32)
            out[...] = part.astype(BF)


def normalize(tokens, gain, order, tile=64):
    layers = len(order)
    rows, features = tokens.shape
    width = features // (4 * layers)
    single = jax.ShapeDtypeStruct((rows, width), BF)
    pair = jax.ShapeDtypeStruct((2, rows, width), BF)
    token, *outs = pl.pallas_call(
        functools.partial(norm_kernel, order, width),
        out_shape=[jax.ShapeDtypeStruct((8, 128), F32)] + [single] * (2 * layers) + [pair] * layers,
        grid=(rows // tile,),
        in_specs=[
            pl.BlockSpec((tile, features), lambda i: (i, 0)),
            pl.BlockSpec((1, features), lambda i: (0, 0)),
        ],
        out_specs=[pl.BlockSpec(memory_space=pl.ANY)]
        + [pl.BlockSpec((tile, width), lambda i: (i, 0))] * (2 * layers)
        + [pl.BlockSpec((2, tile, width), lambda i: (0, i, 0))] * layers,
        compiler_params=pltpu.CompilerParams(vmem_limit_bytes=24 * 2**20),
        name="normalize",
    )(tokens, gain.reshape(1, features))
    return outs[:layers], outs[layers:2 * layers], outs[2 * layers:], token


def whole(shape):
    return pl.BlockSpec(shape, lambda i: (0,) * len(shape))


def at(shape, *where):
    return pl.BlockSpec(shape, lambda i: where)


HELD = pl.BlockSpec(memory_space=pl.ANY)
SCALARS = pl.BlockSpec(memory_space=pltpu.SMEM)


class Line:
    def __init__(self):
        self.token = None

    def run(self, name, jobs, through=(), grid=(1,)):
        n_in = sum(len(ins) for _, ins, _ in jobs)
        held = list(through) + ([] if self.token is None else [self.token])

        def body(*refs):
            outs = refs[n_in + len(held):]
            i = o = 0
            for kernel, ins, made in jobs:
                kernel(*refs[i:i + len(ins)], *outs[o:o + len(made)])
                i, o = i + len(ins), o + len(made)

        made = [out for _, _, outs in jobs for out in outs]
        result = pl.pallas_call(
            body,
            out_shape=[shape for shape, _ in made]
            + [jax.ShapeDtypeStruct(a.shape, a.dtype) for a in through] + [jax.ShapeDtypeStruct((8, 128), F32)],
            grid=grid,
            in_specs=[spec for _, ins, _ in jobs for _, spec in ins] + [HELD] * len(held),
            out_specs=[spec for _, spec in made] + [HELD] * (len(through) + 1),
            input_output_aliases={n_in + i: len(made) + i for i in range(len(through))},
            compiler_params=pltpu.CompilerParams(vmem_limit_bytes=32 * 2**20),
            cost_estimate=pl.CostEstimate(flops=0, bytes_accessed=1, transcendentals=0),
            name=name,
        )(*[a for _, ins, _ in jobs for a, _ in ins], *held)
        self.token = result[-1]
        return result[:len(made)], result[len(made):-1]


def new(shape, dtype=BF):
    return jax.ShapeDtypeStruct(shape, dtype), whole(shape)


def join(pieces):
    def kernel(*refs):
        ins, out = refs[:-1], refs[-1]
        row = 0
        for ref in ins:
            flat = ref.shape[-2:]
            out[row:row + flat[0], :] = ref[...].reshape(flat)
            row += flat[0]

    shape = (sum(block[-2] for _, block, _ in pieces), pieces[0][1][-1])
    return kernel, [(a, at(block, *where)) for a, block, where in pieces], [new(shape)]


def per_device(tokens, gain, kv_weight, block_mask, cotangent):
    group, teams = lax.axis_size("fsdp"), lax.axis_size("tensor")
    layers = group // 4
    rows, features = tokens.shape
    width = features // group
    cols = kv_weight.shape[1]
    flat, one, pair, panel = (rows, width), (1, rows, width), (2 * rows, width), (width, cols)
    mrows, mcols = block_mask.shape
    tall, wide = width // mrows, cols // mcols
    blocks = [
        ((i, j), (slice(i * tall, (i + 1) * tall), slice(j * wide, (j + 1) * wide)))
        for i in range(mrows) for j in range(mcols)
    ]
    order, place = orders(layers)
    line = Line()

    def over_core(a):
        return lax.ppermute(a, "fsdp", [(i, i ^ 1) for i in range(group)])

    def over_x(a):
        return lax.ppermute(a, "fsdp", [(i, i ^ 2) for i in range(group)])

    def over_y(a):
        return [
            lax.ppermute(a, "tensor", [(i, (i + s) % teams) for i in range(teams)])
            for s in range(1, teams)
        ]

    def over_z(a, pairs):
        return lax.ppermute(a, "fsdp", [(4 * p + i, 4 * q + i) for p, q in pairs for i in range(4)])

    def partner(p, side):
        q = p + 1 if p % 2 == side else p - 1
        return q if 0 <= q < layers else p

    def over_edges(a, side):
        return over_z(a, [(p, partner(p, side)) for p in range(layers)])

    own, far, swaps, line.token = normalize(tokens, gain, order)
    swaps = [over_core(a) for a in swaps]

    def near_of(k):
        return [(own[k], flat, (0, 0)), (swaps[k], one, (0, 0, 0))]

    def cross_of(k):
        return [(far[k], flat, (0, 0)), (swaps[k], one, (1, 0, 0))]

    (cross_0, near_0), _ = line.run("first", [join(cross_of(0)), join(near_of(0))])
    cross_0, near_y = over_x(cross_0), over_y(near_0)

    def turn_kernel(a, out):
        for i in range(teams):
            j = lax.rem(spot()[3] + teams - i, teams)
            out[i * rows:(i + 1) * rows, :] = a[pl.ds(pl.multiple_of(j * rows, rows), rows), :]

    def mask_kernel(mask, a, out):
        for spot_in, where in blocks:
            out[where] = (a[where].astype(F32) * mask[spot_in].astype(F32)).astype(BF)

    own_shape, cut = cotangent.shape, (cotangent.shape[0] // 2, cols)
    (cot, masked), _ = line.run(
        "turn_and_mask",
        [
            (turn_kernel, [(cotangent, whole(own_shape))], [new(own_shape)]),
            (mask_kernel, [(block_mask, SCALARS), (kv_weight, whole(panel))], [new(panel)]),
        ],
    )
    cot_x, cot_core = over_x(cot), over_core(cot)
    came = {1: [over_edges(masked, i) for i in range(2)]}

    _, (cross_0, cot_core, *near_y) = line.run("arrived", [], [cross_0, cot_core, *near_y])
    cross_y = over_y(cross_0)
    (near_rest,), _ = line.run("later", [join([p for k in range(1, layers) for p in near_of(k)])])
    (cross_1,), _ = line.run("later", [join(cross_of(1))])
    (rest,), _ = line.run("later", [join([p for k in range(2, layers) for p in cross_of(k)])])
    near_rest_y, cross_1 = over_y(near_rest), over_x(cross_1)

    def split_kernel(a, low, high):
        low[...] = a[:cut[0]]
        high[...] = a[cut[0]:]

    parts, (*cross_y, even, odd) = line.run(
        "split", [(split_kernel, [(cot_x, whole(own_shape))], [new(cut), new(cut)])], [*cross_y, *came[1]]
    )
    came[1] = [even, odd]
    parts = [over_core(part) for part in parts]
    came[2] = [None, over_edges(came[1][0], 1)]
    pieces = [(a, (rows, cols), (i, 0)) for i in range(teams) for a in (cot, cot_core)]
    for i in range(teams):
        pieces.append((cot_x, (rows, cols), (i, 0)))
        pieces.append((parts[2 * i // teams], (rows, cols), (i % (teams // 2), 0)))

    def gather(near, near_y, cross, cross_y, places):
        arrays = [(a, pair, (places[0], 0)) for a in [near, *near_y]]
        return join(arrays + [(a, pair, (places[1], 0)) for a in [cross, *cross_y]])

    def terms_of(a):
        return lax.dot_general(a, cots, (((0,), (0,)), ((), ())), preferred_element_type=F32)

    def going(t, side):
        before, cases = came[t - 1][1 - side], {}
        for p in range(layers):
            q = partner(p, side)
            ahead = layers - 1 - p if q > p else p
            behind = layers - 1 - ahead
            if q == p:
                continue
            if t <= behind + 1:
                cases.setdefault((None, True), []).append(p)
            else:
                far = p + (layers - t + 1) * (q - p)
                cases.setdefault((int(place[p, far]), behind > 0), []).append(p)
        if list(cases) == [(None, True)]:
            return None
        used = [k for k, _ in cases if k is not None]
        ins = [(terms[k], whole(panel)) for k in used] + [(before, whole(panel))]

        def kernel(*refs):
            out = refs[-1]
            for (k, add), layers_of in cases.items():
                @pl.when(functools.reduce(jnp.logical_or, [spot()[0] == p for p in layers_of]))
                def _():
                    if k is None:
                        out[...] = refs[-2][...]
                    elif add:
                        out[...] = (refs[used.index(k)][...] + refs[-2][...].astype(F32)).astype(BF)
                    else:
                        out[...] = refs[used.index(k)][...].astype(BF)

        return kernel, ins, [new(panel)]

    def phase(t, sides, through=()):
        jobs = [going(t, i) for i in sides]
        made, through = line.run("phase", [job for job in jobs if job], through)
        made = list(made)
        came.setdefault(t, [None, None])
        for i, job in zip(sides, jobs):
            came[t][i] = over_edges(made.pop(0) if job else came[t - 1][1 - i], i)
        return through

    (cots, normed_0), _ = line.run("head", [join(pieces), gather(near_0, near_y, cross_0, cross_y, (0, 0))])
    normed, terms = [normed_0], [terms_of(normed_0)]
    phase(2, [0])
    _, (cross_1, rest, *near_rest_y) = line.run("arrived", [], [cross_1, rest, *near_rest_y])
    cross_1_y, rest = over_y(cross_1), over_x(rest)
    (normed_1,), _ = line.run("rows", [gather(near_rest, near_rest_y, cross_1, cross_1_y, (0, 0))])
    normed.append(normed_1)
    terms.append(terms_of(normed_1))
    phase(3, [0, 1])
    if layers > 3:
        rest, _ = line.run("arrived", [join([(rest, pair, (k, 0))]) for k in range(layers - 2)])
    rest_y = [over_y(a) for a in rest]
    more, _ = line.run(
        "rows",
        [gather(near_rest, near_rest_y, rest[k - 2], rest_y[k - 2], (k - 1, 0)) for k in range(2, layers)],
    )
    normed += more
    terms += [terms_of(a) for a in more]
    for t in range(4, layers + 1):
        phase(t, [0, 1])

    def choose(k):
        cases = {}
        for i in range(layers):
            d = int(order[i, k])
            cases.setdefault((abs(d - i), (i - 1 if d < i else i) % 2 if d != i else 0), []).append(i)

        def kernel(*refs):
            out = refs[-1]
            for n, layers_of in enumerate(cases.values()):
                def copy(n=n):
                    out[...] = refs[n][...]

                if len(cases) == 1:
                    copy()
                else:
                    pl.when(functools.reduce(jnp.logical_or, [spot()[0] == i for i in layers_of]))(copy)

        return kernel, [(came[s][i] if s else masked, whole(panel)) for s, i in cases], [new(panel)]

    weight, _ = line.run("weights", [choose(k) for k in range(layers)])

    half = max(teams // 2, 1)
    part = (half * rows, cols)

    def project(side, h):
        def kernel(*refs):
            rows_of, weights, keep, send = refs[:layers], refs[layers:2 * layers], refs[-2], refs[-1]
            total = jnp.dot(rows_of[0][...], weights[0][...], preferred_element_type=F32)
            for k in range(1, layers):
                total += jnp.dot(rows_of[k][...], weights[k][...], preferred_element_type=F32)
            keep[...] = total[:rows]
            send[...] = total[rows:].astype(BF)

        ins = [(n, pl.BlockSpec(pair, lambda i: (side * teams + h * half + i, 0))) for n in normed]
        ins += [(w, whole(panel)) for w in weight]
        outs = [
            (jax.ShapeDtypeStruct(part, d), pl.BlockSpec((rows, cols), lambda i: (i, 0))) for d in (F32, BF)
        ]
        kept, sent = line.run("project", [(kernel, ins, outs)], grid=(half,))[0]
        return kept, over_core(sent)

    def add_kernel(kept, sent, out):
        out[...] = (kept[...] + sent[...].astype(F32)).astype(BF)

    halves = range(teams // half)
    theirs = [project(1, h) for h in halves]
    arrived = []
    mine = []
    for h in halves:
        (a,), _ = line.run("cross_sum", [(add_kernel, [(a, whole(part)) for a in theirs[h]], [new(part)])])
        arrived.append(over_x(a))
        mine.append(project(0, h))

    def own_kernel(mask, term, even, odd, out):
        z = spot()[0]
        last = [jnp.where((z > 0) & (z < layers - 1), 1.0, 0.0).astype(F32), jnp.float32(1)]
        for spot_in, where in blocks:
            total = term[where]
            for i, a in enumerate([even, odd]):
                alone = partner(0, i) == 0
                total += a[where].astype(F32) * last[0] if alone else a[where].astype(F32)
            out[where] = total * mask[spot_in].astype(F32)

    ins = [(block_mask, SCALARS)] + [(a, whole(panel)) for a in [terms[layers - 1], *came[layers]]]
    (weight_grad,), _ = line.run("own_gradient", [(own_kernel, ins, [new(panel, F32)])])

    def last_sum(*refs):
        out = refs[-1]
        for h in halves:
            kept, sent, a = refs[3 * h:3 * h + 3]
            total = (kept[...] + sent[...].astype(F32) + a[...].astype(F32)).astype(BF)
            for i in range(half):
                j = lax.rem(spot()[3] + teams - h * half - i, teams)
                out[pl.ds(pl.multiple_of(j * rows, rows), rows), :] = total[i * rows:(i + 1) * rows]

    ins = [(a, whole(part)) for h in halves for a in (*mine[h], arrived[h])]
    (projected,), _ = line.run("projected", [(last_sum, ins, [new((teams * rows, cols))])])
    return (projected, weight_grad)


def solution(mesh):
    return jax.shard_map(
        per_device,
        mesh=mesh,
        in_specs=(
            P(("fsdp", "tensor"), None),
            P(),
            P("fsdp", "tensor"),
            P("fsdp", "tensor"),
            P("fsdp", "tensor"),
        ),
        out_specs=(P("fsdp", "tensor"), P("fsdp", "tensor")),
        check_vma=False,
    )
```

```python
import functools

import jax
import jax.numpy as jnp
import numpy as np
from jax import lax
from jax.experimental import pallas as pl
from jax.experimental.pallas import tpu as pltpu
from jax.sharding import PartitionSpec as P

BF = jnp.bfloat16
F32 = jnp.float32


def orders(depth):
    def rank(z):
        return lambda d: (-abs(d - z), abs(2 * d - depth + 1))

    order = np.array([sorted(range(depth), key=rank(z)) for z in range(depth)])
    return order, np.argsort(order, axis=1)


def lookup(table, where):
    out = jnp.int32(int(table[0]))
    for i in range(1, len(table)):
        out = jnp.where(where == i, jnp.int32(int(table[i])), out)
    return out


def lookup(table, where):
    out = jnp.int32(int(table[0]))
    for i in range(1, len(table)):
        out = jnp.where(where == i, jnp.int32(int(table[i])), out)
    return out


def spot():
    f = lax.axis_index("fsdp")
    return lax.div(f, 4), lax.rem(lax.div(f, 2), 2), lax.rem(f, 2), lax.axis_index("tensor")


def norm_kernel(order, width, tokens, gain, token, *outs):
    layers = len(order)
    z, x, c, _ = spot()
    values = tokens[...].astype(F32)
    scale = lax.rsqrt(jnp.mean(values * values, axis=-1, keepdims=True) + 1e-05)
    for k in range(layers):
        own, far, swap = outs[k], outs[layers + k], outs[2 * layers + k]
        layer = lookup(order[:, k], z) * 4
        for out, rx, rc in [(own, 0, 0), (swap.at[0], 0, 1), (far, 1, 0), (swap.at[1], 1, 1)]:
            place = layer + jnp.bitwise_xor(x, rx) * 2 + jnp.bitwise_xor(c, rc)
            at = pl.ds(pl.multiple_of(place * width, width), width)
            part = tokens[:, at].astype(F32) * scale * gain[:, at].astype(F32)
            out[...] = part.astype(BF)


def normalize(tokens, gain, order, tile=64):
    layers = len(order)
    rows, features = tokens.shape
    width = features // (4 * layers)
    single = jax.ShapeDtypeStruct((rows, width), BF)
    pair = jax.ShapeDtypeStruct((2, rows, width), BF)
    token, *outs = pl.pallas_call(
        functools.partial(norm_kernel, order, width),
        out_shape=[jax.ShapeDtypeStruct((8, 128), F32)] + [single] * (2 * layers) + [pair] * layers,
        grid=(rows // tile,),
        in_specs=[
            pl.BlockSpec((tile, features), lambda i: (i, 0)),
            pl.BlockSpec((1, features), lambda i: (0, 0)),
        ],
        out_specs=[pl.BlockSpec(memory_space=pl.ANY)]
        + [pl.BlockSpec((tile, width), lambda i: (i, 0))] * (2 * layers)
        + [pl.BlockSpec((2, tile, width), lambda i: (0, i, 0))] * layers,
        compiler_params=pltpu.CompilerParams(vmem_limit_bytes=24 * 2**20),
        name="normalize",
    )(tokens, gain.reshape(1, features))
    return outs[:layers], outs[layers:2 * layers], outs[2 * layers:], token


def whole(shape):
    return pl.BlockSpec(shape, lambda i: (0,) * len(shape))


def at(shape, *where):
    return pl.BlockSpec(shape, lambda i: where)


HELD = pl.BlockSpec(memory_space=pl.ANY)
SCALARS = pl.BlockSpec(memory_space=pltpu.SMEM)


class Line:
    def __init__(self):
        self.token = None

    def run(self, name, jobs, through=(), grid=(1,)):
        n_in = sum(len(ins) for _, ins, _ in jobs)
        held = list(through) + ([] if self.token is None else [self.token])

        def body(*refs):
            outs = refs[n_in + len(held):]
            i = o = 0
            for kernel, ins, made in jobs:
                kernel(*refs[i:i + len(ins)], *outs[o:o + len(made)])
                i, o = i + len(ins), o + len(made)

        made = [out for _, _, outs in jobs for out in outs]
        result = pl.pallas_call(
            body,
            out_shape=[shape for shape, _ in made]
            + [jax.ShapeDtypeStruct(a.shape, a.dtype) for a in through] + [jax.ShapeDtypeStruct((8, 128), F32)],
            grid=grid,
            in_specs=[spec for _, ins, _ in jobs for _, spec in ins] + [HELD] * len(held),
            out_specs=[spec for _, spec in made] + [HELD] * (len(through) + 1),
            input_output_aliases={n_in + i: len(made) + i for i in range(len(through))},
            compiler_params=pltpu.CompilerParams(vmem_limit_bytes=32 * 2**20),
            cost_estimate=pl.CostEstimate(flops=0, bytes_accessed=1, transcendentals=0),
            name=name,
        )(*[a for _, ins, _ in jobs for a, _ in ins], *held)
        self.token = result[-1]
        return result[:len(made)], result[len(made):-1]


def new(shape, dtype=BF):
    return jax.ShapeDtypeStruct(shape, dtype), whole(shape)


def join(pieces):
    def kernel(*refs):
        ins, out = refs[:-1], refs[-1]
        row = 0
        for ref in ins:
            flat = ref.shape[-2:]
            out[row:row + flat[0], :] = ref[...].reshape(flat)
            row += flat[0]

    shape = (sum(block[-2] for _, block, _ in pieces), pieces[0][1][-1])
    return kernel, [(a, at(block, *where)) for a, block, where in pieces], [new(shape)]


def per_device(tokens, gain, kv_weight, block_mask, cotangent):
    group, teams = lax.axis_size("fsdp"), lax.axis_size("tensor")
    layers = group // 4
    rows, features = tokens.shape
    width = features // group
    cols = kv_weight.shape[1]
    flat, one, pair, panel = (rows, width), (1, rows, width), (2 * rows, width), (width, cols)
    mrows, mcols = block_mask.shape
    tall, wide = width // mrows, cols // mcols
    blocks = [
        ((i, j), (slice(i * tall, (i + 1) * tall), slice(j * wide, (j + 1) * wide)))
        for i in range(mrows) for j in range(mcols)
    ]
    order, place = orders(layers)
    line = Line()

    def over_core(a):
        return lax.ppermute(a, "fsdp", [(i, i ^ 1) for i in range(group)])

    def over_x(a):
        return lax.ppermute(a, "fsdp", [(i, i ^ 2) for i in range(group)])

    def over_y(a):
        return [
            lax.ppermute(a, "tensor", [(i, (i + s) % teams) for i in range(teams)])
            for s in range(1, teams)
        ]

    def over_z(a, pairs):
        return lax.ppermute(a, "fsdp", [(4 * p + i, 4 * q + i) for p, q in pairs for i in range(4)])

    def partner(p, side):
        q = p + 1 if p % 2 == side else p - 1
        return q if 0 <= q < layers else p

    def over_edges(a, side):
        return over_z(a, [(p, partner(p, side)) for p in range(layers)])

    own, far, swaps, line.token = normalize(tokens, gain, order)
    swaps = [over_core(a) for a in swaps]

    def near_of(k):
        return [(own[k], flat, (0, 0)), (swaps[k], one, (0, 0, 0))]

    def cross_of(k):
        return [(far[k], flat, (0, 0)), (swaps[k], one, (1, 0, 0))]

    (cross_0, near_0), _ = line.run("first", [join(cross_of(0)), join(near_of(0))])
    cross_0, near_y = over_x(cross_0), over_y(near_0)

    def turn_kernel(a, out):
        for i in range(teams):
            j = lax.rem(spot()[3] + teams - i, teams)
            out[i * rows:(i + 1) * rows, :] = a[pl.ds(pl.multiple_of(j * rows, rows), rows), :]

    def mask_kernel(mask, a, out):
        for spot_in, where in blocks:
            out[where] = (a[where].astype(F32) * mask[spot_in].astype(F32)).astype(BF)

    own_shape, cut = cotangent.shape, (cotangent.shape[0] // 2, cols)
    (cot, masked), _ = line.run(
        "turn_and_mask",
        [
            (turn_kernel, [(cotangent, whole(own_shape))], [new(own_shape)]),
            (mask_kernel, [(block_mask, SCALARS), (kv_weight, whole(panel))], [new(panel)]),
        ],
    )
    cot_x, cot_core = over_x(cot), over_core(cot)
    came = {1: [over_edges(masked, i) for i in range(2)]}

    _, (cross_0, cot_core, *near_y) = line.run("arrived", [], [cross_0, cot_core, *near_y])
    cross_y = over_y(cross_0)
    (near_rest,), _ = line.run("later", [join([p for k in range(1, layers) for p in near_of(k)])])
    (cross_1,), _ = line.run("later", [join(cross_of(1))])
    (rest,), _ = line.run("later", [join([p for k in range(2, layers) for p in cross_of(k)])])
    near_rest_y, cross_1 = over_y(near_rest), over_x(cross_1)

    def split_kernel(a, low, high):
        low[...] = a[:cut[0]]
        high[...] = a[cut[0]:]

    parts, (*cross_y, even, odd) = line.run(
        "split", [(split_kernel, [(cot_x, whole(own_shape))], [new(cut), new(cut)])], [*cross_y, *came[1]]
    )
    came[1] = [even, odd]
    parts = [over_core(part) for part in parts]
    came[2] = [None, over_edges(came[1][0], 1)]
    pieces = [(a, (rows, cols), (i, 0)) for i in range(teams) for a in (cot, cot_core)]
    for i in range(teams):
        pieces.append((cot_x, (rows, cols), (i, 0)))
        pieces.append((parts[2 * i // teams], (rows, cols), (i % (teams // 2), 0)))

    def gather(near, near_y, cross, cross_y, places):
        arrays = [(a, pair, (places[0], 0)) for a in [near, *near_y]]
        return join(arrays + [(a, pair, (places[1], 0)) for a in [cross, *cross_y]])

    def terms_of(a):
        return lax.dot_general(a, cots, (((0,), (0,)), ((), ())), preferred_element_type=F32)

    def going(t, side):
        before, cases = came[t - 1][1 - side], {}
        for p in range(layers):
            q = partner(p, side)
            ahead = layers - 1 - p if q > p else p
            behind = layers - 1 - ahead
            if q == p:
                continue
            if t <= behind + 1:
                cases.setdefault((None, True), []).append(p)
            else:
                far = p + (layers - t + 1) * (q - p)
                cases.setdefault((int(place[p, far]), behind > 0), []).append(p)
        if list(cases) == [(None, True)]:
            return None
        used = [k for k, _ in cases if k is not None]
        ins = [(terms[k], whole(panel)) for k in used] + [(before, whole(panel))]

        def kernel(*refs):
            out = refs[-1]
            for (k, add), layers_of in cases.items():
                @pl.when(functools.reduce(jnp.logical_or, [spot()[0] == p for p in layers_of]))
                def _():
                    if k is None:
                        out[...] = refs[-2][...]
                    elif add:
                        out[...] = (refs[used.index(k)][...] + refs[-2][...].astype(F32)).astype(BF)
                    else:
                        out[...] = refs[used.index(k)][...].astype(BF)

        return kernel, ins, [new(panel)]

    def phase(t, sides, through=()):
        jobs = [going(t, i) for i in sides]
        made, through = line.run("phase", [job for job in jobs if job], through)
        made = list(made)
        came.setdefault(t, [None, None])
        for i, job in zip(sides, jobs):
            came[t][i] = over_edges(made.pop(0) if job else came[t - 1][1 - i], i)
        return through

    (cots, normed_0), _ = line.run("head", [join(pieces), gather(near_0, near_y, cross_0, cross_y, (0, 0))])
    normed, terms = [normed_0], [terms_of(normed_0)]
    phase(2, [0])
    _, (cross_1, rest, *near_rest_y) = line.run("arrived", [], [cross_1, rest, *near_rest_y])
    cross_1_y, rest = over_y(cross_1), over_x(rest)
    (normed_1,), _ = line.run("rows", [gather(near_rest, near_rest_y, cross_1, cross_1_y, (0, 0))])
    normed.append(normed_1)
    terms.append(terms_of(normed_1))
    phase(3, [0, 1])
    if layers > 3:
        rest, _ = line.run("arrived", [join([(rest, pair, (k, 0))]) for k in range(layers - 2)])
    rest_y = [over_y(a) for a in rest]
    more, _ = line.run(
        "rows",
        [gather(near_rest, near_rest_y, rest[k - 2], rest_y[k - 2], (k - 1, 0)) for k in range(2, layers)],
    )
    normed += more
    terms += [terms_of(a) for a in more]
    for t in range(4, layers + 1):
        phase(t, [0, 1])

    def choose(k):
        cases = {}
        for i in range(layers):
            d = int(order[i, k])
            cases.setdefault((abs(d - i), (i - 1 if d < i else i) % 2 if d != i else 0), []).append(i)

        def kernel(*refs):
            out = refs[-1]
            for n, layers_of in enumerate(cases.values()):
                def copy(n=n):
                    out[...] = refs[n][...]

                if len(cases) == 1:
                    copy()
                else:
                    pl.when(functools.reduce(jnp.logical_or, [spot()[0] == i for i in layers_of]))(copy)

        return kernel, [(came[s][i] if s else masked, whole(panel)) for s, i in cases], [new(panel)]

    weight, _ = line.run("weights", [choose(k) for k in range(layers)])

    half = max(teams // 2, 1)
    part = (half * rows, cols)

    def project(side, h):
        def kernel(*refs):
            rows_of, weights, keep, send = refs[:layers], refs[layers:2 * layers], refs[-2], refs[-1]
            total = jnp.dot(rows_of[0][...], weights[0][...], preferred_element_type=F32)
            for k in range(1, layers):
                total += jnp.dot(rows_of[k][...], weights[k][...], preferred_element_type=F32)
            keep[...] = total[:rows]
            send[...] = total[rows:].astype(BF)

        ins = [(n, pl.BlockSpec(pair, lambda i: (side * teams + h * half + i, 0))) for n in normed]
        ins += [(w, whole(panel)) for w in weight]
        outs = [
            (jax.ShapeDtypeStruct(part, d), pl.BlockSpec((rows, cols), lambda i: (i, 0))) for d in (F32, BF)
        ]
        kept, sent = line.run("project", [(kernel, ins, outs)], grid=(half,))[0]
        return kept, over_core(sent)

    def add_kernel(kept, sent, out):
        out[...] = (kept[...] + sent[...].astype(F32)).astype(BF)

    halves = range(teams // half)
    theirs = [project(1, h) for h in halves]
    arrived = []
    mine = []
    for h in halves:
        (a,), (terms[-1],) = line.run(
            "cross_sum", [(add_kernel, [(a, whole(part)) for a in theirs[h]], [new(part)])], [terms[-1]]
        )
        arrived.append(over_x(a))
        mine.append(project(0, h))

    def own_kernel(mask, term, even, odd, out):
        z = spot()[0]
        last = [jnp.where((z > 0) & (z < layers - 1), 1.0, 0.0).astype(F32), jnp.float32(1)]
        for spot_in, where in blocks:
            total = term[where]
            for i, a in enumerate([even, odd]):
                alone = partner(0, i) == 0
                total += a[where].astype(F32) * last[0] if alone else a[where].astype(F32)
            out[where] = total * mask[spot_in].astype(F32)

    ins = [(block_mask, SCALARS)] + [(a, whole(panel)) for a in [terms[layers - 1], *came[layers]]]
    (weight_grad,), _ = line.run("own_gradient", [(own_kernel, ins, [new(panel, F32)])])

    def last_sum(*refs):
        out = refs[-1]
        for h in halves:
            kept, sent, a = refs[3 * h:3 * h + 3]
            total = (kept[...] + sent[...].astype(F32) + a[...].astype(F32)).astype(BF)
            for i in range(half):
                j = lax.rem(spot()[3] + teams - h * half - i, teams)
                out[pl.ds(pl.multiple_of(j * rows, rows), rows), :] = total[i * rows:(i + 1) * rows]

    ins = [(a, whole(part)) for h in halves for a in (*mine[h], arrived[h])]
    (projected,), _ = line.run("projected", [(last_sum, ins, [new((teams * rows, cols))])])
    return (projected, weight_grad)


def solution(mesh):
    return jax.shard_map(
        per_device,
        mesh=mesh,
        in_specs=(
            P(("fsdp", "tensor"), None),
            P(),
            P("fsdp", "tensor"),
            P("fsdp", "tensor"),
            P("fsdp", "tensor"),
        ),
        out_specs=(P("fsdp", "tensor"), P("fsdp", "tensor")),
        check_vma=False,
    )
```

```python
import functools

import jax
import jax.numpy as jnp
import numpy as np
from jax import lax
from jax.experimental import pallas as pl
from jax.experimental.pallas import tpu as pltpu
from jax.sharding import PartitionSpec as P

BF = jnp.bfloat16
F32 = jnp.float32


def orders(depth):
    def rank(z):
        return lambda d: (-abs(d - z), abs(2 * d - depth + 1))

    order = np.array([sorted(range(depth), key=rank(z)) for z in range(depth)])
    return order, np.argsort(order, axis=1)


def lookup(table, where):
    out = jnp.int32(int(table[0]))
    for i in range(1, len(table)):
        out = jnp.where(where == i, jnp.int32(int(table[i])), out)
    return out


def lookup(table, where):
    out = jnp.int32(int(table[0]))
    for i in range(1, len(table)):
        out = jnp.where(where == i, jnp.int32(int(table[i])), out)
    return out


def spot():
    f = lax.axis_index("fsdp")
    return lax.div(f, 4), lax.rem(lax.div(f, 2), 2), lax.rem(f, 2), lax.axis_index("tensor")


def norm_kernel(order, width, tokens, gain, token, *outs):
    layers = len(order)
    z, x, c, _ = spot()
    values = tokens[...].astype(F32)
    scale = lax.rsqrt(jnp.mean(values * values, axis=-1, keepdims=True) + 1e-05)
    for k in range(layers):
        own, far, swap = outs[k], outs[layers + k], outs[2 * layers + k]
        layer = lookup(order[:, k], z) * 4
        for out, rx, rc in [(own, 0, 0), (swap.at[0], 0, 1), (far, 1, 0), (swap.at[1], 1, 1)]:
            place = layer + jnp.bitwise_xor(x, rx) * 2 + jnp.bitwise_xor(c, rc)
            at = pl.ds(pl.multiple_of(place * width, width), width)
            part = tokens[:, at].astype(F32) * scale * gain[:, at].astype(F32)
            out[...] = part.astype(BF)


def normalize(tokens, gain, order, tile=64):
    layers = len(order)
    rows, features = tokens.shape
    width = features // (4 * layers)
    single = jax.ShapeDtypeStruct((rows, width), BF)
    pair = jax.ShapeDtypeStruct((2, rows, width), BF)
    token, *outs = pl.pallas_call(
        functools.partial(norm_kernel, order, width),
        out_shape=[jax.ShapeDtypeStruct((8, 128), F32)] + [single] * (2 * layers) + [pair] * layers,
        grid=(rows // tile,),
        in_specs=[
            pl.BlockSpec((tile, features), lambda i: (i, 0)),
            pl.BlockSpec((1, features), lambda i: (0, 0)),
        ],
        out_specs=[pl.BlockSpec(memory_space=pl.ANY)]
        + [pl.BlockSpec((tile, width), lambda i: (i, 0))] * (2 * layers)
        + [pl.BlockSpec((2, tile, width), lambda i: (0, i, 0))] * layers,
        compiler_params=pltpu.CompilerParams(vmem_limit_bytes=24 * 2**20),
        name="normalize",
    )(tokens, gain.reshape(1, features))
    return outs[:layers], outs[layers:2 * layers], outs[2 * layers:], token


def whole(shape):
    return pl.BlockSpec(shape, lambda i: (0,) * len(shape))


def at(shape, *where):
    return pl.BlockSpec(shape, lambda i: where)


HELD = pl.BlockSpec(memory_space=pl.ANY)
SCALARS = pl.BlockSpec(memory_space=pltpu.SMEM)


class Line:
    def __init__(self):
        self.token = None

    def run(self, name, jobs, through=(), grid=(1,)):
        n_in = sum(len(ins) for _, ins, _ in jobs)
        held = list(through) + ([] if self.token is None else [self.token])

        def body(*refs):
            outs = refs[n_in + len(held):]
            i = o = 0
            for kernel, ins, made in jobs:
                kernel(*refs[i:i + len(ins)], *outs[o:o + len(made)])
                i, o = i + len(ins), o + len(made)

        made = [out for _, _, outs in jobs for out in outs]
        result = pl.pallas_call(
            body,
            out_shape=[shape for shape, _ in made]
            + [jax.ShapeDtypeStruct(a.shape, a.dtype) for a in through] + [jax.ShapeDtypeStruct((8, 128), F32)],
            grid=grid,
            in_specs=[spec for _, ins, _ in jobs for _, spec in ins] + [HELD] * len(held),
            out_specs=[spec for _, spec in made] + [HELD] * (len(through) + 1),
            input_output_aliases={n_in + i: len(made) + i for i in range(len(through))},
            compiler_params=pltpu.CompilerParams(vmem_limit_bytes=32 * 2**20),
            cost_estimate=pl.CostEstimate(flops=0, bytes_accessed=1, transcendentals=0),
            name=name,
        )(*[a for _, ins, _ in jobs for a, _ in ins], *held)
        self.token = result[-1]
        return result[:len(made)], result[len(made):-1]


def new(shape, dtype=BF):
    return jax.ShapeDtypeStruct(shape, dtype), whole(shape)


def join(pieces):
    def kernel(*refs):
        ins, out = refs[:-1], refs[-1]
        row = 0
        for ref in ins:
            flat = ref.shape[-2:]
            out[row:row + flat[0], :] = ref[...].reshape(flat)
            row += flat[0]

    shape = (sum(block[-2] for _, block, _ in pieces), pieces[0][1][-1])
    return kernel, [(a, at(block, *where)) for a, block, where in pieces], [new(shape)]


def per_device(tokens, gain, kv_weight, block_mask, cotangent):
    group, teams = lax.axis_size("fsdp"), lax.axis_size("tensor")
    layers = group // 4
    rows, features = tokens.shape
    width = features // group
    cols = kv_weight.shape[1]
    flat, one, pair, panel = (rows, width), (1, rows, width), (2 * rows, width), (width, cols)
    mrows, mcols = block_mask.shape
    tall, wide = width // mrows, cols // mcols
    blocks = [
        ((i, j), (slice(i * tall, (i + 1) * tall), slice(j * wide, (j + 1) * wide)))
        for i in range(mrows) for j in range(mcols)
    ]
    order, place = orders(layers)
    line = Line()

    def over_core(a):
        return lax.ppermute(a, "fsdp", [(i, i ^ 1) for i in range(group)])

    def over_x(a):
        return lax.ppermute(a, "fsdp", [(i, i ^ 2) for i in range(group)])

    def over_y(a):
        return [
            lax.ppermute(a, "tensor", [(i, (i + s) % teams) for i in range(teams)])
            for s in range(1, teams)
        ]

    def over_z(a, pairs):
        return lax.ppermute(a, "fsdp", [(4 * p + i, 4 * q + i) for p, q in pairs for i in range(4)])

    def partner(p, side):
        q = p + 1 if p % 2 == side else p - 1
        return q if 0 <= q < layers else p

    def over_edges(a, side):
        return over_z(a, [(p, partner(p, side)) for p in range(layers)])

    own, far, swaps, line.token = normalize(tokens, gain, order)
    swaps = [over_core(a) for a in swaps]

    def near_of(k):
        return [(own[k], flat, (0, 0)), (swaps[k], one, (0, 0, 0))]

    def cross_of(k):
        return [(far[k], flat, (0, 0)), (swaps[k], one, (1, 0, 0))]

    (cross_0, near_0), _ = line.run("first", [join(cross_of(0)), join(near_of(0))])
    cross_0, near_y = over_x(cross_0), over_y(near_0)

    def turn_kernel(a, out):
        for i in range(teams):
            j = lax.rem(spot()[3] + teams - i, teams)
            out[i * rows:(i + 1) * rows, :] = a[pl.ds(pl.multiple_of(j * rows, rows), rows), :]

    def mask_kernel(mask, a, out):
        for spot_in, where in blocks:
            out[where] = (a[where].astype(F32) * mask[spot_in].astype(F32)).astype(BF)

    own_shape, cut = cotangent.shape, (cotangent.shape[0] // 2, cols)
    (cot, masked), _ = line.run(
        "turn_and_mask",
        [
            (turn_kernel, [(cotangent, whole(own_shape))], [new(own_shape)]),
            (mask_kernel, [(block_mask, SCALARS), (kv_weight, whole(panel))], [new(panel)]),
        ],
    )
    cot_x, cot_core = over_x(cot), over_core(cot)
    came = {1: [over_edges(masked, i) for i in range(2)]}

    _, (cross_0, cot_core, *near_y) = line.run("arrived", [], [cross_0, cot_core, *near_y])
    cross_y = over_y(cross_0)
    (near_rest,), _ = line.run("later", [join([p for k in range(1, layers) for p in near_of(k)])])
    (cross_1,), _ = line.run("later", [join(cross_of(1))])
    (rest,), _ = line.run("later", [join([p for k in range(2, layers) for p in cross_of(k)])])
    near_rest_y, cross_1 = over_y(near_rest), over_x(cross_1)

    def split_kernel(a, low, high):
        low[...] = a[:cut[0]]
        high[...] = a[cut[0]:]

    parts, (*cross_y, even, odd) = line.run(
        "split", [(split_kernel, [(cot_x, whole(own_shape))], [new(cut), new(cut)])], [*cross_y, *came[1]]
    )
    came[1] = [even, odd]
    parts = [over_core(part) for part in parts]
    came[2] = [None, over_edges(came[1][0], 1)]
    pieces = [(a, (rows, cols), (i, 0)) for i in range(teams) for a in (cot, cot_core)]
    for i in range(teams):
        pieces.append((cot_x, (rows, cols), (i, 0)))
        pieces.append((parts[2 * i // teams], (rows, cols), (i % (teams // 2), 0)))

    def gather(near, near_y, cross, cross_y, places):
        arrays = [(a, pair, (places[0], 0)) for a in [near, *near_y]]
        return join(arrays + [(a, pair, (places[1], 0)) for a in [cross, *cross_y]])

    def terms_of(a):
        return lax.dot_general(a, cots, (((0,), (0,)), ((), ())), preferred_element_type=F32)

    def going(t, side):
        before, cases = came[t - 1][1 - side], {}
        for p in range(layers):
            q = partner(p, side)
            ahead = layers - 1 - p if q > p else p
            behind = layers - 1 - ahead
            if q == p:
                continue
            if t <= behind + 1:
                cases.setdefault((None, True), []).append(p)
            else:
                far = p + (layers - t + 1) * (q - p)
                cases.setdefault((int(place[p, far]), behind > 0), []).append(p)
        if list(cases) == [(None, True)]:
            return None
        used = [k for k, _ in cases if k is not None]
        ins = [(terms[k], whole(panel)) for k in used] + [(before, whole(panel))]

        def kernel(*refs):
            out = refs[-1]
            for (k, add), layers_of in cases.items():
                @pl.when(functools.reduce(jnp.logical_or, [spot()[0] == p for p in layers_of]))
                def _():
                    if k is None:
                        out[...] = refs[-2][...]
                    elif add:
                        out[...] = (refs[used.index(k)][...] + refs[-2][...].astype(F32)).astype(BF)
                    else:
                        out[...] = refs[used.index(k)][...].astype(BF)

        return kernel, ins, [new(panel)]

    def phase(t, sides, through=()):
        jobs = [going(t, i) for i in sides]
        made, through = line.run("phase", [job for job in jobs if job], through)
        made = list(made)
        came.setdefault(t, [None, None])
        for i, job in zip(sides, jobs):
            came[t][i] = over_edges(made.pop(0) if job else came[t - 1][1 - i], i)
        return through

    (cots, normed_0), _ = line.run("head", [join(pieces), gather(near_0, near_y, cross_0, cross_y, (0, 0))])
    normed, terms = [normed_0], [terms_of(normed_0)]
    phase(2, [0])
    _, (cross_1, rest) = line.run("arrived", [], [cross_1, rest])
    rest = over_x(rest)
    _, (cross_1, *near_rest_y) = line.run("arrived", [], [cross_1, *near_rest_y])
    cross_1_y = over_y(cross_1)
    (normed_1,), _ = line.run("rows", [gather(near_rest, near_rest_y, cross_1, cross_1_y, (0, 0))])
    normed.append(normed_1)
    terms.append(terms_of(normed_1))
    phase(3, [0, 1])
    if layers > 3:
        rest, _ = line.run("arrived", [join([(rest, pair, (k, 0))]) for k in range(layers - 2)])
    rest_y = [over_y(a) for a in rest]
    more, _ = line.run(
        "rows",
        [gather(near_rest, near_rest_y, rest[k - 2], rest_y[k - 2], (k - 1, 0)) for k in range(2, layers)],
    )
    normed += more
    terms += [terms_of(a) for a in more]
    for t in range(4, layers + 1):
        phase(t, [0, 1])

    def choose(k):
        cases = {}
        for i in range(layers):
            d = int(order[i, k])
            cases.setdefault((abs(d - i), (i - 1 if d < i else i) % 2 if d != i else 0), []).append(i)

        def kernel(*refs):
            out = refs[-1]
            for n, layers_of in enumerate(cases.values()):
                def copy(n=n):
                    out[...] = refs[n][...]

                if len(cases) == 1:
                    copy()
                else:
                    pl.when(functools.reduce(jnp.logical_or, [spot()[0] == i for i in layers_of]))(copy)

        return kernel, [(came[s][i] if s else masked, whole(panel)) for s, i in cases], [new(panel)]

    weight, _ = line.run("weights", [choose(k) for k in range(layers)])

    half = max(teams // 2, 1)
    part = (half * rows, cols)

    def project(side, h):
        def kernel(*refs):
            rows_of, weights, keep, send = refs[:layers], refs[layers:2 * layers], refs[-2], refs[-1]
            total = jnp.dot(rows_of[0][...], weights[0][...], preferred_element_type=F32)
            for k in range(1, layers):
                total += jnp.dot(rows_of[k][...], weights[k][...], preferred_element_type=F32)
            keep[...] = total[:rows]
            send[...] = total[rows:].astype(BF)

        ins = [(n, pl.BlockSpec(pair, lambda i: (side * teams + h * half + i, 0))) for n in normed]
        ins += [(w, whole(panel)) for w in weight]
        outs = [
            (jax.ShapeDtypeStruct(part, d), pl.BlockSpec((rows, cols), lambda i: (i, 0))) for d in (F32, BF)
        ]
        kept, sent = line.run("project", [(kernel, ins, outs)], grid=(half,))[0]
        return kept, over_core(sent)

    halves = range(teams // half)
    theirs = [project(1, h) for h in halves]

    def sum_kernel(*refs):
        out = refs[-1]
        for h in halves:
            out[h * half * rows:(h + 1) * half * rows, :] = (refs[2 * h][...] + refs[2 * h + 1][...].astype(F32)).astype(BF)

    (a,), (terms[-1],) = line.run(
        "cross_sum",
        [(sum_kernel, [(a, whole(part)) for h in halves for a in theirs[h]], [new((teams * rows, cols))])],
        [terms[-1]],
    )
    arrived = over_x(a)
    mine = [project(0, h) for h in halves]

    def own_kernel(mask, term, even, odd, out):
        z = spot()[0]
        last = [jnp.where((z > 0) & (z < layers - 1), 1.0, 0.0).astype(F32), jnp.float32(1)]
        for spot_in, where in blocks:
            total = term[where]
            for i, a in enumerate([even, odd]):
                alone = partner(0, i) == 0
                total += a[where].astype(F32) * last[0] if alone else a[where].astype(F32)
            out[where] = total * mask[spot_in].astype(F32)

    ins = [(block_mask, SCALARS)] + [(a, whole(panel)) for a in [terms[layers - 1], *came[layers]]]
    (weight_grad,), _ = line.run("own_gradient", [(own_kernel, ins, [new(panel, F32)])])

    held = [*normed, cots]
    for _ in range(1):
        _, held = line.run("spacer", [], held)

    def last_sum(*refs):
        out = refs[-1]
        for h in halves:
            kept, sent = refs[2 * h:2 * h + 2]
            came_x = refs[-2][h * half * rows:(h + 1) * half * rows, :].astype(F32)
            total = (kept[...] + sent[...].astype(F32) + came_x).astype(BF)
            for i in range(half):
                j = lax.rem(spot()[3] + teams - h * half - i, teams)
                out[pl.ds(pl.multiple_of(j * rows, rows), rows), :] = total[i * rows:(i + 1) * rows]

    ins = [(a, whole(part)) for h in halves for a in mine[h]] + [(arrived, whole((teams * rows, cols)))]
    (projected,), _ = line.run("projected", [(last_sum, ins, [new((teams * rows, cols))])])
    return (projected, weight_grad)


def solution(mesh):
    return jax.shard_map(
        per_device,
        mesh=mesh,
        in_specs=(
            P(("fsdp", "tensor"), None),
            P(),
            P("fsdp", "tensor"),
            P("fsdp", "tensor"),
            P("fsdp", "tensor"),
        ),
        out_specs=(P("fsdp", "tensor"), P("fsdp", "tensor")),
        check_vma=False,
    )
```

```python
import functools

import jax
import jax.numpy as jnp
import numpy as np
from jax import lax
from jax.experimental import pallas as pl
from jax.experimental.pallas import tpu as pltpu
from jax.sharding import PartitionSpec as P

BF = jnp.bfloat16
F32 = jnp.float32


def orders(depth):
    def rank(z):
        return lambda d: (-abs(d - z), abs(2 * d - depth + 1))

    order = np.array([sorted(range(depth), key=rank(z)) for z in range(depth)])
    return order, np.argsort(order, axis=1)


def lookup(table, where):
    out = jnp.int32(int(table[0]))
    for i in range(1, len(table)):
        out = jnp.where(where == i, jnp.int32(int(table[i])), out)
    return out


def lookup(table, where):
    out = jnp.int32(int(table[0]))
    for i in range(1, len(table)):
        out = jnp.where(where == i, jnp.int32(int(table[i])), out)
    return out


def spot():
    f = lax.axis_index("fsdp")
    return lax.div(f, 4), lax.rem(lax.div(f, 2), 2), lax.rem(f, 2), lax.axis_index("tensor")


def norm_kernel(order, width, tokens, gain, token, *outs):
    layers = len(order)
    z, x, c, _ = spot()
    values = tokens[...].astype(F32)
    scale = lax.rsqrt(jnp.mean(values * values, axis=-1, keepdims=True) + 1e-05)
    for k in range(layers):
        own, far, swap = outs[k], outs[layers + k], outs[2 * layers + k]
        layer = lookup(order[:, k], z) * 4
        for out, rx, rc in [(own, 0, 0), (swap.at[0], 0, 1), (far, 1, 0), (swap.at[1], 1, 1)]:
            place = layer + jnp.bitwise_xor(x, rx) * 2 + jnp.bitwise_xor(c, rc)
            at = pl.ds(pl.multiple_of(place * width, width), width)
            part = tokens[:, at].astype(F32) * scale * gain[:, at].astype(F32)
            out[...] = part.astype(BF)


def normalize(tokens, gain, order, tile=64):
    layers = len(order)
    rows, features = tokens.shape
    width = features // (4 * layers)
    single = jax.ShapeDtypeStruct((rows, width), BF)
    pair = jax.ShapeDtypeStruct((2, rows, width), BF)
    token, *outs = pl.pallas_call(
        functools.partial(norm_kernel, order, width),
        out_shape=[jax.ShapeDtypeStruct((8, 128), F32)] + [single] * (2 * layers) + [pair] * layers,
        grid=(rows // tile,),
        in_specs=[
            pl.BlockSpec((tile, features), lambda i: (i, 0)),
            pl.BlockSpec((1, features), lambda i: (0, 0)),
        ],
        out_specs=[pl.BlockSpec(memory_space=pl.ANY)]
        + [pl.BlockSpec((tile, width), lambda i: (i, 0))] * (2 * layers)
        + [pl.BlockSpec((2, tile, width), lambda i: (0, i, 0))] * layers,
        compiler_params=pltpu.CompilerParams(vmem_limit_bytes=24 * 2**20),
        name="normalize",
    )(tokens, gain.reshape(1, features))
    return outs[:layers], outs[layers:2 * layers], outs[2 * layers:], token


def whole(shape):
    return pl.BlockSpec(shape, lambda i: (0,) * len(shape))


def at(shape, *where):
    return pl.BlockSpec(shape, lambda i: where)


HELD = pl.BlockSpec(memory_space=pl.ANY)
SCALARS = pl.BlockSpec(memory_space=pltpu.SMEM)


class Line:
    def __init__(self):
        self.token = None

    def run(self, name, jobs, through=(), grid=(1,)):
        n_in = sum(len(ins) for _, ins, _ in jobs)
        held = list(through) + ([] if self.token is None else [self.token])

        def body(*refs):
            outs = refs[n_in + len(held):]
            i = o = 0
            for kernel, ins, made in jobs:
                kernel(*refs[i:i + len(ins)], *outs[o:o + len(made)])
                i, o = i + len(ins), o + len(made)

        made = [out for _, _, outs in jobs for out in outs]
        result = pl.pallas_call(
            body,
            out_shape=[shape for shape, _ in made]
            + [jax.ShapeDtypeStruct(a.shape, a.dtype) for a in through] + [jax.ShapeDtypeStruct((8, 128), F32)],
            grid=grid,
            in_specs=[spec for _, ins, _ in jobs for _, spec in ins] + [HELD] * len(held),
            out_specs=[spec for _, spec in made] + [HELD] * (len(through) + 1),
            input_output_aliases={n_in + i: len(made) + i for i in range(len(through))},
            compiler_params=pltpu.CompilerParams(vmem_limit_bytes=32 * 2**20),
            cost_estimate=pl.CostEstimate(flops=0, bytes_accessed=1, transcendentals=0),
            name=name,
        )(*[a for _, ins, _ in jobs for a, _ in ins], *held)
        self.token = result[-1]
        return result[:len(made)], result[len(made):-1]


def new(shape, dtype=BF):
    return jax.ShapeDtypeStruct(shape, dtype), whole(shape)


def join(pieces):
    def kernel(*refs):
        ins, out = refs[:-1], refs[-1]
        row = 0
        for ref in ins:
            flat = ref.shape[-2:]
            out[row:row + flat[0], :] = ref[...].reshape(flat)
            row += flat[0]

    shape = (sum(block[-2] for _, block, _ in pieces), pieces[0][1][-1])
    return kernel, [(a, at(block, *where)) for a, block, where in pieces], [new(shape)]


def per_device(tokens, gain, kv_weight, block_mask, cotangent):
    group, teams = lax.axis_size("fsdp"), lax.axis_size("tensor")
    layers = group // 4
    rows, features = tokens.shape
    width = features // group
    cols = kv_weight.shape[1]
    flat, one, pair, panel = (rows, width), (1, rows, width), (2 * rows, width), (width, cols)
    mrows, mcols = block_mask.shape
    tall, wide = width // mrows, cols // mcols
    blocks = [
        ((i, j), (slice(i * tall, (i + 1) * tall), slice(j * wide, (j + 1) * wide)))
        for i in range(mrows) for j in range(mcols)
    ]
    order, place = orders(layers)
    line = Line()

    def over_core(a):
        return lax.ppermute(a, "fsdp", [(i, i ^ 1) for i in range(group)])

    def over_x(a):
        return lax.ppermute(a, "fsdp", [(i, i ^ 2) for i in range(group)])

    def over_y(a):
        return [
            lax.ppermute(a, "tensor", [(i, (i + s) % teams) for i in range(teams)])
            for s in range(1, teams)
        ]

    def over_z(a, pairs):
        return lax.ppermute(a, "fsdp", [(4 * p + i, 4 * q + i) for p, q in pairs for i in range(4)])

    def partner(p, side):
        q = p + 1 if p % 2 == side else p - 1
        return q if 0 <= q < layers else p

    def over_edges(a, side):
        return over_z(a, [(p, partner(p, side)) for p in range(layers)])

    own, far, swaps, line.token = normalize(tokens, gain, order)
    swaps = [over_core(a) for a in swaps]

    def near_of(k):
        return [(own[k], flat, (0, 0)), (swaps[k], one, (0, 0, 0))]

    def cross_of(k):
        return [(far[k], flat, (0, 0)), (swaps[k], one, (1, 0, 0))]

    def turn_kernel(a, out):
        for i in range(teams):
            j = lax.rem(spot()[3] + teams - i, teams)
            out[i * rows:(i + 1) * rows, :] = a[pl.ds(pl.multiple_of(j * rows, rows), rows), :]

    def mask_kernel(mask, a, out):
        for spot_in, where in blocks:
            out[where] = (a[where].astype(F32) * mask[spot_in].astype(F32)).astype(BF)

    own_shape, cut = cotangent.shape, (cotangent.shape[0] // 2, cols)
    (cot, masked), _ = line.run(
        "turn_and_mask",
        [
            (turn_kernel, [(cotangent, whole(own_shape))], [new(own_shape)]),
            (mask_kernel, [(block_mask, SCALARS), (kv_weight, whole(panel))], [new(panel)]),
        ],
    )
    cot_x, cot_core = over_x(cot), over_core(cot)
    (cross_0, near_0), _ = line.run("first", [join(cross_of(0)), join(near_of(0))])
    cross_0, near_y = over_x(cross_0), over_y(near_0)
    came = {1: [over_edges(masked, i) for i in range(2)]}

    _, (cross_0, cot_core, *near_y) = line.run("arrived", [], [cross_0, cot_core, *near_y])
    cross_y = over_y(cross_0)
    (near_rest,), _ = line.run("later", [join([p for k in range(1, layers) for p in near_of(k)])])
    (cross_1,), _ = line.run("later", [join(cross_of(1))])
    (rest,), _ = line.run("later", [join([p for k in range(2, layers) for p in cross_of(k)])])
    near_rest_y, cross_1 = over_y(near_rest), over_x(cross_1)

    def split_kernel(a, low, high):
        low[...] = a[:cut[0]]
        high[...] = a[cut[0]:]

    parts, (*cross_y, even, odd) = line.run(
        "split", [(split_kernel, [(cot_x, whole(own_shape))], [new(cut), new(cut)])], [*cross_y, *came[1]]
    )
    came[1] = [even, odd]
    parts = [over_core(part) for part in parts]
    came[2] = [None, over_edges(came[1][0], 1)]
    pieces = [(a, (rows, cols), (i, 0)) for i in range(teams) for a in (cot, cot_core)]
    for i in range(teams):
        pieces.append((cot_x, (rows, cols), (i, 0)))
        pieces.append((parts[2 * i // teams], (rows, cols), (i % (teams // 2), 0)))

    def gather(near, near_y, cross, cross_y, places):
        arrays = [(a, pair, (places[0], 0)) for a in [near, *near_y]]
        return join(arrays + [(a, pair, (places[1], 0)) for a in [cross, *cross_y]])

    def terms_of(a):
        return lax.dot_general(a, cots, (((0,), (0,)), ((), ())), preferred_element_type=F32)

    def going(t, side):
        before, cases = came[t - 1][1 - side], {}
        for p in range(layers):
            q = partner(p, side)
            ahead = layers - 1 - p if q > p else p
            behind = layers - 1 - ahead
            if q == p:
                continue
            if t <= behind + 1:
                cases.setdefault((None, True), []).append(p)
            else:
                far = p + (layers - t + 1) * (q - p)
                cases.setdefault((int(place[p, far]), behind > 0), []).append(p)
        if list(cases) == [(None, True)]:
            return None
        used = [k for k, _ in cases if k is not None]
        ins = [(terms[k], whole(panel)) for k in used] + [(before, whole(panel))]

        def kernel(*refs):
            out = refs[-1]
            for (k, add), layers_of in cases.items():
                @pl.when(functools.reduce(jnp.logical_or, [spot()[0] == p for p in layers_of]))
                def _():
                    if k is None:
                        out[...] = refs[-2][...]
                    elif add:
                        out[...] = (refs[used.index(k)][...] + refs[-2][...].astype(F32)).astype(BF)
                    else:
                        out[...] = refs[used.index(k)][...].astype(BF)

        return kernel, ins, [new(panel)]

    def phase(t, sides, through=()):
        jobs = [going(t, i) for i in sides]
        made, through = line.run("phase", [job for job in jobs if job], through)
        made = list(made)
        came.setdefault(t, [None, None])
        for i, job in zip(sides, jobs):
            came[t][i] = over_edges(made.pop(0) if job else came[t - 1][1 - i], i)
        return through

    (cots, normed_0), _ = line.run("head", [join(pieces), gather(near_0, near_y, cross_0, cross_y, (0, 0))])
    normed, terms = [normed_0], [terms_of(normed_0)]
    phase(2, [0])
    _, (cross_1, rest) = line.run("arrived", [], [cross_1, rest])
    rest = over_x(rest)
    _, (cross_1, *near_rest_y) = line.run("arrived", [], [cross_1, *near_rest_y])
    cross_1_y = over_y(cross_1)
    (normed_1,), _ = line.run("rows", [gather(near_rest, near_rest_y, cross_1, cross_1_y, (0, 0))])
    normed.append(normed_1)
    terms.append(terms_of(normed_1))
    phase(3, [0, 1])
    if layers > 3:
        rest, _ = line.run("arrived", [join([(rest, pair, (k, 0))]) for k in range(layers - 2)])
    rest_y = [over_y(a) for a in rest]
    more, _ = line.run(
        "rows",
        [gather(near_rest, near_rest_y, rest[k - 2], rest_y[k - 2], (k - 1, 0)) for k in range(2, layers)],
    )
    normed += more
    terms += [terms_of(a) for a in more]
    for t in range(4, layers + 1):
        phase(t, [0, 1])

    def choose(k):
        cases = {}
        for i in range(layers):
            d = int(order[i, k])
            cases.setdefault((abs(d - i), (i - 1 if d < i else i) % 2 if d != i else 0), []).append(i)

        def kernel(*refs):
            out = refs[-1]
            for n, layers_of in enumerate(cases.values()):
                def copy(n=n):
                    out[...] = refs[n][...]

                if len(cases) == 1:
                    copy()
                else:
                    pl.when(functools.reduce(jnp.logical_or, [spot()[0] == i for i in layers_of]))(copy)

        return kernel, [(came[s][i] if s else masked, whole(panel)) for s, i in cases], [new(panel)]

    weight, _ = line.run("weights", [choose(k) for k in range(layers)])

    half = max(teams // 2, 1)
    part = (half * rows, cols)

    def project(side, h):
        def kernel(*refs):
            rows_of, weights, keep, send = refs[:layers], refs[layers:2 * layers], refs[-2], refs[-1]
            total = jnp.dot(rows_of[0][...], weights[0][...], preferred_element_type=F32)
            for k in range(1, layers):
                total += jnp.dot(rows_of[k][...], weights[k][...], preferred_element_type=F32)
            keep[...] = total[:rows]
            send[...] = total[rows:].astype(BF)

        ins = [(n, pl.BlockSpec(pair, lambda i: (side * teams + h * half + i, 0))) for n in normed]
        ins += [(w, whole(panel)) for w in weight]
        outs = [
            (jax.ShapeDtypeStruct(part, d), pl.BlockSpec((rows, cols), lambda i: (i, 0))) for d in (F32, BF)
        ]
        kept, sent = line.run("project", [(kernel, ins, outs)], grid=(half,))[0]
        return kept, over_core(sent)

    halves = range(teams // half)
    theirs = [project(1, h) for h in halves]

    def sum_kernel(*refs):
        out = refs[-1]
        for h in halves:
            out[h * half * rows:(h + 1) * half * rows, :] = (refs[2 * h][...] + refs[2 * h + 1][...].astype(F32)).astype(BF)

    (a,), (terms[-1],) = line.run(
        "cross_sum",
        [(sum_kernel, [(a, whole(part)) for h in halves for a in theirs[h]], [new((teams * rows, cols))])],
        [terms[-1]],
    )
    arrived = over_x(a)
    mine = [project(0, h) for h in halves]

    def own_kernel(mask, term, even, odd, out):
        z = spot()[0]
        last = [jnp.where((z > 0) & (z < layers - 1), 1.0, 0.0).astype(F32), jnp.float32(1)]
        for spot_in, where in blocks:
            total = term[where]
            for i, a in enumerate([even, odd]):
                alone = partner(0, i) == 0
                total += a[where].astype(F32) * last[0] if alone else a[where].astype(F32)
            out[where] = total * mask[spot_in].astype(F32)

    ins = [(block_mask, SCALARS)] + [(a, whole(panel)) for a in [terms[layers - 1], *came[layers]]]
    (weight_grad,), _ = line.run("own_gradient", [(own_kernel, ins, [new(panel, F32)])])

    held = [*normed, cots]
    for _ in range(1):
        _, held = line.run("spacer", [], held)

    def last_sum(*refs):
        out = refs[-1]
        for h in halves:
            kept, sent = refs[2 * h:2 * h + 2]
            came_x = refs[-2][h * half * rows:(h + 1) * half * rows, :].astype(F32)
            total = (kept[...] + sent[...].astype(F32) + came_x).astype(BF)
            for i in range(half):
                j = lax.rem(spot()[3] + teams - h * half - i, teams)
                out[pl.ds(pl.multiple_of(j * rows, rows), rows), :] = total[i * rows:(i + 1) * rows]

    ins = [(a, whole(part)) for h in halves for a in mine[h]] + [(arrived, whole((teams * rows, cols)))]
    (projected,), _ = line.run("projected", [(last_sum, ins, [new((teams * rows, cols))])])
    return (projected, weight_grad)


def solution(mesh):
    return jax.shard_map(
        per_device,
        mesh=mesh,
        in_specs=(
            P(("fsdp", "tensor"), None),
            P(),
            P("fsdp", "tensor"),
            P("fsdp", "tensor"),
            P("fsdp", "tensor"),
        ),
        out_specs=(P("fsdp", "tensor"), P("fsdp", "tensor")),
        check_vma=False,
    )
```
